512 devices in a mesh: grp: 8 (over y_lo, core), tile: 64 (over y_hi, x, z).
Axes of the slice: x: 4, y: 8 (y_hi: 2, y_lo: 4; y = y_hi * 4 + y_lo), z: 8, core: 2. Of those that a mesh axis runs over, the one named last changes fastest.
Arguments:
- hidden: bfloat16 [8, 512, 128, 128], P('grp', 'tile'), may hold values from -13 to 13
- cotangent: float32 [8, 512, 128], P('grp', 'tile'), may hold values from -16 to 16
- spectral_w: bfloat16 [4096, 256], P('tile'), may hold values from -0.375 to 0.375
- conv_k: float32 [9, 128], replicated, may hold values from -2 to 2
- proj_w: float32 [128], replicated, may hold values from -0.5 to 0.5
Outputs:
- grad_hidden: float32 [8, 512, 128, 128], P('grp', 'tile')
- grad_spectral: float32 [4096, 256], P('tile')
- grad_conv: float32 [9, 128], replicated
- grad_proj: float32 [128], replicated
The draws below stay inside these ranges and needn't reach their ends.
All inputs are finite; a program needn't handle non-finite values.
Results may differ from the reference program's by a relative error of at most 0.015.
Values may be sent and summed in bfloat16 or wider, within the bound.
No kernel may reach another device: no remote copies, remote signals or barrier semaphores. Data moves between devices by JAX's collectives and lax.ppermute only.
A program may use at most 64 MiB of HBM per device.

```python
import jax
import jax.numpy as jnp
from jax import lax

BINS = 128
CH = 128
MODES = 32
NX = 8
NY = 512


def draw_hidden(key, part):
    key_base, key_scale = jax.random.split(jax.random.fold_in(key, 11))
    base = jnp.clip(jax.random.normal(key_base, (NX, NY, BINS, CH), jnp.float32), -4.0, 4.0)
    scale = jnp.exp(jax.random.uniform(key_scale, (NX, NY, 1, 1), jnp.float32, -1.15, 1.15))
    return (base * scale).astype(jnp.bfloat16)


def draw_cotangent(key, part):
    key_base = jax.random.fold_in(key, 23)
    column = jnp.arange(NY, dtype=jnp.float32) / max(NY - 1, 1)
    base = jnp.clip(jax.random.normal(key_base, (NX, NY, BINS), jnp.float32), -4.0, 4.0)
    ramp = 1.0 + 2.0 * column
    return base * ramp[None, :, None]


def block_scale(stream_key, extent, cuts, least, top_value):
    def one(axis_at, shards_of):
        heights = jax.random.uniform(jax.random.fold_in(jax.random.fold_in(stream_key, 6), axis_at), (shards_of,), jnp.float32, least / len(cuts), top_value / len(cuts))
        return jnp.repeat(jnp.exp(heights), extent[axis_at] // shards_of).reshape((-1,) + (1,) * (len(extent) - axis_at - 1))

    factor_of = one(*cuts[0])
    for cut in cuts[1:]:
        factor_of = factor_of * one(*cut)
    return factor_of


def normal_values(own_key, dims, deviation, reach, cuts=(), held_as=jnp.bfloat16):
    values = deviation * jax.random.normal(own_key, dims, jnp.float32)
    if cuts:
        values = values * block_scale(own_key, dims, cuts, -0.22, 0.18)
    return jnp.clip(values, -reach, reach).astype(held_as)


def setup_inputs(seed: int = 0) -> dict:
    streams_of = jax.random.split(jax.random.key(seed), 6)
    hidden = draw_hidden(jax.random.fold_in(streams_of[5], 71), 0)
    cotangent = draw_cotangent(jax.random.fold_in(streams_of[5], 71), 0)
    spectral_w = normal_values(streams_of[2], (MODES * CH, 2 * CH), (2 * CH) ** -0.5, 0.375, ((0, 64),))
    conv_k = normal_values(streams_of[3], (9, CH), 9 ** -0.5, 2.0, (), jnp.float32)
    proj_w = normal_values(streams_of[4], (CH,), CH ** -0.5, 0.5, (), jnp.float32)
    return dict(hidden=hidden, cotangent=cotangent, spectral_w=spectral_w, conv_k=conv_k, proj_w=proj_w)


HIGH = lax.Precision.HIGHEST


def spectral_tables(modes, bins):
    mode_idx = jnp.arange(modes, dtype=jnp.int32)
    bin_idx = jnp.arange(bins, dtype=jnp.int32)
    phase_int = (mode_idx[:, None] * bin_idx[None, :]) % bins
    angle_val = phase_int.astype(jnp.float32) * (2.0 * jnp.pi / bins)
    cosine = jnp.cos(angle_val)
    sine = jnp.sin(angle_val)
    forward_tab = jnp.concatenate([cosine, -sine], 0).astype(jnp.bfloat16)
    weight_k = jnp.where(mode_idx == 0, 1.0, 2.0).astype(jnp.float32)[:, None] / bins
    inverse_tab = jnp.concatenate([cosine * weight_k, -sine * weight_k], 0).T.astype(jnp.bfloat16)
    return forward_tab, inverse_tab


def build_mixer(weights, modes, chans):
    real_w = weights[:, :chans].reshape(modes, chans, chans)
    imag_w = weights[:, chans:].reshape(modes, chans, chans)
    upper = jnp.concatenate([real_w, imag_w], 2)
    lower = jnp.concatenate([-imag_w, real_w], 2)
    return jnp.concatenate([upper, lower], 1)


def gelu_pair(value):
    normal_cdf = 0.5 * (1.0 + jax.scipy.special.erf(value * 0.7071067811865476))
    return value * normal_cdf, normal_cdf + value * jnp.exp(-0.5 * value * value) * 0.3989422804014327


def widen(value):
    return value.astype(jnp.float32)


def cell_backward(hidden_cells, local_term, cot_cells, mixer, forward_tab, inverse_tab, proj_w):
    modes = mixer.shape[0]
    chans = proj_w.shape[0]
    spec_h = jnp.einsum("jb,pbc->jpc", widen(forward_tab), widen(hidden_cells), precision=HIGH).astype(jnp.bfloat16)
    h_cat = jnp.concatenate([spec_h[:modes], spec_h[modes:]], 2)
    mixed = jnp.einsum("kpa,kab->kpb", widen(h_cat), widen(mixer), precision=HIGH).astype(jnp.bfloat16)
    mixed_stack = jnp.concatenate([mixed[:, :, :chans], mixed[:, :, chans:]], 0)
    spectral_out = jnp.einsum("bj,jpo->pbo", widen(inverse_tab), widen(mixed_stack), precision=HIGH)
    pre_act = spectral_out + local_term
    activ, slope = gelu_pair(pre_act)
    proj_grad = jnp.einsum("pb,pbo->o", cot_cells, activ, precision=HIGH)
    grad_pre = (cot_cells[:, :, None] * proj_w * slope).astype(jnp.bfloat16)
    grad_mix = jnp.einsum("bj,pbo->jpo", widen(inverse_tab), widen(grad_pre), precision=HIGH).astype(jnp.bfloat16)
    grad_real = grad_mix[:modes]
    grad_imag = grad_mix[modes:]
    grad_cat = jnp.concatenate([grad_real, grad_imag], 2)
    grad_spec = jnp.einsum("kpb,kab->kpa", widen(grad_cat), widen(mixer), precision=HIGH).astype(jnp.bfloat16)
    grad_stack = jnp.concatenate([grad_spec[:, :, :chans], grad_spec[:, :, chans:]], 0)
    grad_in = jnp.einsum("jb,jpc->pbc", widen(forward_tab), widen(grad_stack), precision=HIGH)
    left_side = jnp.concatenate([spec_h[:modes], spec_h[modes:]], 1)
    right_side = jnp.concatenate([grad_cat, jnp.concatenate([grad_imag, -grad_real], 2)], 1)
    weight_term = jnp.einsum("kpc,kpo->kco", widen(left_side), widen(right_side), precision=HIGH).reshape(modes * chans, 2 * chans)
    return grad_pre, grad_in, weight_term, proj_grad


def reference(hidden, cotangent, spectral_w, conv_k, proj_w):
    forward_tab, inverse_tab = spectral_tables(MODES, BINS)
    mixer = build_mixer(spectral_w, MODES, CH)
    x_pad = jnp.pad(hidden, ((1, 1), (1, 1), (0, 0), (0, 0)))
    offsets = [(row_off, col_off) for row_off in (-1, 0, 1) for col_off in (-1, 0, 1)]

    def one_row(carry, index_row):
        x_rows = lax.dynamic_slice_in_dim(x_pad, index_row, 3, 0)
        center = lax.dynamic_index_in_dim(hidden, index_row, 0, keepdims=False)
        cot_cells = lax.dynamic_index_in_dim(cotangent, index_row, 0, keepdims=False)
        shifted = [x_rows[1 + row_off, 1 + col_off:1 + col_off + NY].astype(jnp.float32) for row_off, col_off in offsets]
        local_term = shifted[0] * conv_k[0]
        for index_d in range(1, 9):
            local_term = local_term + shifted[index_d] * conv_k[index_d]
        grad_pre, grad_in, weight_term, proj_grad = cell_backward(center, local_term, cot_cells, mixer, forward_tab, inverse_tab, proj_w)
        pre_wide = grad_pre.astype(jnp.float32)
        conv_part = jnp.stack([jnp.sum(item * pre_wide, (0, 1)) for item in shifted], 0)
        weight_sum, conv_sum, proj_sum = carry
        return (weight_sum + weight_term, conv_sum + conv_part, proj_sum + proj_grad), (grad_pre, grad_in)

    init = (jnp.zeros((MODES * CH, 2 * CH), jnp.float32), jnp.zeros((9, CH), jnp.float32), jnp.zeros((CH,), jnp.float32))
    row_ids = jnp.arange(NX, dtype=jnp.int32)
    carry, (grad_pre_all, grad_in_all) = lax.scan(one_row, init, row_ids)
    grad_pad = jnp.pad(grad_pre_all, ((1, 1), (1, 1), (0, 0), (0, 0)))

    def out_row(state, inputs):
        index_row, grad_in_row = inputs
        g_rows = lax.dynamic_slice_in_dim(grad_pad, index_row, 3, 0)
        total = grad_in_row
        for index_d, (row_off, col_off) in enumerate(offsets):
            total = total + g_rows[1 - row_off, 1 - col_off:1 - col_off + NY].astype(jnp.float32) * conv_k[index_d]
        return state, total

    _, grad_hidden = lax.scan(out_row, jnp.zeros((), jnp.float32), (row_ids, grad_in_all))
    weight_grad, conv_grad, proj_total = carry
    return grad_hidden, weight_grad, conv_grad, proj_total
```

```python
import jax
import jax.numpy as jnp
from jax import lax
from jax.sharding import PartitionSpec as P

BF = jnp.bfloat16
F32 = jnp.float32


def padded(block, axis, dim):
    count = lax.axis_size(axis)
    forward = [(i, i + 1) for i in range(count - 1)]
    backward = [(target, source) for source, target in forward]
    low = lax.ppermute(
        lax.slice_in_dim(block, block.shape[dim] - 1, None, axis=dim), axis, forward
    )
    high = lax.ppermute(lax.slice_in_dim(block, 0, 1, axis=dim), axis, backward)
    return low, high


def spectral_tables(modes, bins):
    mode_idx = jnp.arange(modes, dtype=jnp.int32)
    bin_idx = jnp.arange(bins, dtype=jnp.int32)
    phase_int = mode_idx[:, None] * bin_idx[None, :] % bins
    angle_val = phase_int.astype(F32) * (2.0 * jnp.pi / bins)
    cosine = jnp.cos(angle_val)
    sine = jnp.sin(angle_val)
    forward_tab = jnp.concatenate([cosine, -sine], 0).astype(BF)
    weight_k = jnp.where(mode_idx == 0, 1.0, 2.0).astype(F32)[:, None] / bins
    inverse_tab = jnp.concatenate([cosine * weight_k, -sine * weight_k], 0).T.astype(BF)
    return (forward_tab, inverse_tab)


def gelu_pair(value):
    normal_cdf = 0.5 * (1.0 + jax.scipy.special.erf(value * 0.7071067811865476))
    return (
        value * normal_cdf,
        normal_cdf + value * jnp.exp(-0.5 * value * value) * 0.3989422804014327,
    )


def split3(value):
    top = lax.reduce_precision(value, 8, 7)
    rest = value - top
    mid = lax.reduce_precision(rest, 8, 7)
    return jnp.stack([top, mid, rest - mid], 0).astype(BF)


def exchange(value, axis):
    return lax.all_to_all(value, axis, 0, 0, tiled=True)


def tied(*values):
    return lax.optimization_barrier(values)


def local(hidden, cotangent, spectral_w, conv_k, proj_w):
    rows_here, cols, bins, chans = hidden.shape
    groups = lax.axis_size("grp")
    tiles = lax.axis_size("tile")
    half = spectral_w.shape[0]
    modes = half * tiles // chans
    parts = chans // half
    cells = rows_here * cols
    forward_tab, inverse_tab = spectral_tables(modes, bins)
    real_w = spectral_w[:, :chans]
    imag_w = spectral_w[:, chans:]
    mixer = jnp.concatenate(
        [jnp.concatenate([real_w, imag_w], 1), jnp.concatenate([-imag_w, real_w], 1)], 0
    )
    block = hidden.reshape(cells, bins, chans)
    low_t, high_t = padded(hidden, "tile", 1)
    spec_h = jnp.einsum("jb,pbc->jpc", forward_tab, block, preferred_element_type=F32).astype(BF)
    sent = (
        spec_h.reshape(2, modes, cells, parts, half)
        .transpose(1, 3, 2, 0, 4)
        .reshape(tiles, cells, 2 * half)
    )
    got_h = exchange(sent, "tile")
    got_h, low_t, high_t = tied(got_h, low_t, high_t)
    wide = jnp.concatenate([low_t, hidden, high_t], 1)
    low_g, high_g = padded(wide, "grp", 0)
    own_h = got_h.reshape(tiles * cells, 2 * half)
    part = jnp.dot(own_h, mixer, preferred_element_type=F32).astype(BF)
    back = exchange(part.reshape(tiles, cells, 2 * chans), "tile")
    back, low_g, high_g, wide = tied(back, low_g, high_g, wide)
    x_pad = jnp.concatenate([low_g, wide, high_g], 0)
    inverse_twice = jnp.broadcast_to(
        inverse_tab.reshape(bins, 2, modes).transpose(0, 2, 1)[:, :, None, :],
        (bins, modes, parts, 2),
    )
    spectral_out = jnp.einsum(
        "bkhr,khpro->pbo",
        inverse_twice,
        back.reshape(modes, parts, cells, 2, chans),
        preferred_element_type=F32,
    )
    offsets = [(row_off, col_off) for row_off in (-1, 0, 1) for col_off in (-1, 0, 1)]
    local_term = jnp.zeros((rows_here, cols, bins, chans), F32)
    for index_d, (row_off, col_off) in enumerate(offsets):
        window = x_pad[1 + row_off : 1 + row_off + rows_here, 1 + col_off : 1 + col_off + cols]
        local_term = local_term + window.astype(F32) * conv_k[index_d]
    pre_act = spectral_out + local_term.reshape(cells, bins, chans)
    activ, slope = gelu_pair(pre_act)
    cot_cells = cotangent.reshape(cells, bins, 1)
    proj_part = jnp.sum(cot_cells * activ, (0, 1))
    grad_pre = (cot_cells * proj_w * slope).astype(BF)
    grad_block = grad_pre.reshape(rows_here, cols, bins, chans)
    low_gt, high_gt = padded(grad_block, "tile", 1)
    wide_grad = grad_block.astype(F32)
    sums = [
        jnp.sum(
            x_pad[
                1 + row_off : 1 + row_off + rows_here, 1 + col_off : 1 + col_off + cols
            ].astype(F32)
            * wide_grad,
            (0, 1, 2),
        )
        for row_off, col_off in offsets
    ] + [proj_part]
    count = len(sums)
    piece = count * chans // tiles
    small = split3(jnp.stack(sums, 0)).reshape(3, tiles, piece).transpose(1, 0, 2)
    small = jnp.pad(small.reshape(tiles, 3 * piece), ((0, 0), (0, chans - 3 * piece)))
    small = jnp.pad(small[:, None, :], ((0, 0), (0, cells - 1), (0, 0)))
    grad_mix = jnp.einsum("bj,pbo->jpo", inverse_tab, grad_pre, preferred_element_type=F32).astype(BF)
    grad_sent = grad_mix.reshape(2, modes, cells, chans).transpose(1, 2, 0, 3)
    grad_sent = jnp.broadcast_to(
        grad_sent.reshape(modes, 1, cells, 2 * chans), (modes, parts, cells, 2 * chans)
    )
    grad_sent = jnp.concatenate([grad_sent.reshape(tiles, cells, 2 * chans), small], 2)
    got_g = exchange(grad_sent, "tile")
    got_g, low_gt, high_gt = tied(got_g, low_gt, high_gt)
    grad_wide = jnp.concatenate([low_gt, grad_block, high_gt], 1)
    low_gg, high_gg = padded(grad_wide, "grp", 0)
    own_g = got_g[:, :, : 2 * chans].reshape(tiles * cells, 2 * chans)
    small_sum = jnp.sum(got_g[:, 0, 2 * chans : 2 * chans + 3 * piece].astype(F32), 0)
    small_sum = split3(small_sum.reshape(3, piece).sum(0)).reshape(1, 1, 3 * piece)
    small_sum = jnp.pad(small_sum, ((0, 0), (0, cells - 1), (0, 2 * half - 3 * piece)))
    small_sum = jnp.broadcast_to(small_sum, (tiles, cells, 2 * half))
    grad_spec = lax.dot_general(
        own_g, mixer, (((1,), (1,)), ((), ())), preferred_element_type=F32
    ).astype(BF)
    spec_sent = jnp.concatenate([grad_spec.reshape(tiles, cells, 2 * half), small_sum], 2)
    cross = lax.dot_general(own_h, own_g, (((0,), (0,)), ((), ())), preferred_element_type=F32)
    weight_part = jnp.concatenate(
        [
            cross[:half, :chans] + cross[half:, chans:],
            cross[:half, chans:] - cross[half:, :chans],
        ],
        1,
    ).astype(BF)
    got_s = exchange(spec_sent, "tile")
    got_s, low_gg, high_gg, weight_part = tied(got_s, low_gg, high_gg, weight_part)
    totals = got_s[:, 0, 2 * half : 2 * half + 3 * piece].reshape(tiles, 3, piece)
    totals = totals.transpose(1, 0, 2).reshape(3 * count * chans // (2 * chans), 2 * chans)
    last = jnp.concatenate([weight_part, totals], 0)
    last = exchange(jnp.broadcast_to(last, (groups,) + last.shape), "grp")
    grad_spectral = jnp.sum(last[:, :half].astype(F32), 0)
    totals = last[:, half:].astype(F32).reshape(groups, 3, count, chans)
    totals = jnp.sum(totals, (0, 1))
    grad_stack = (
        got_s[:, :, : 2 * half]
        .reshape(modes, parts, cells, 2, half)
        .transpose(3, 0, 2, 1, 4)
        .reshape(2 * modes, cells, chans)
    )
    grad_in = jnp.einsum("jb,jpc->pbc", forward_tab, grad_stack, preferred_element_type=F32)
    grad_pad = jnp.concatenate([low_gg, grad_wide, high_gg], 0)
    grad_hidden = grad_in.reshape(rows_here, cols, bins, chans)
    for index_d, (row_off, col_off) in enumerate(offsets):
        window = grad_pad[1 - row_off : 1 - row_off + rows_here, 1 - col_off : 1 - col_off + cols]
        grad_hidden = grad_hidden + window.astype(F32) * conv_k[index_d]
    return (grad_hidden, grad_spectral, totals[: count - 1], totals[count - 1])


def solution(mesh):
    in_specs = (P("grp", "tile", None, None), P("grp", "tile", None), P("tile", None), P(), P())
    out_specs = (P("grp", "tile", None, None), P("tile", None), P(), P())
    return jax.shard_map(local, mesh=mesh, in_specs=in_specs, out_specs=out_specs, check_vma=False)
```

```python
import jax
import jax.numpy as jnp
import numpy as np
from jax import lax
from jax.experimental import pallas as pl
from jax.experimental.pallas import tpu as pltpu
from jax.sharding import PartitionSpec as P

BF = jnp.bfloat16
F32 = jnp.float32


def shifted(block, axis, step):
    count = lax.axis_size(axis)
    pairs = [(i, i + step) for i in range(count) if 0 <= i + step < count]
    return lax.ppermute(block, axis, pairs)


def edge_pack(columns, cot):
    flat = columns.reshape(-1, columns.shape[-1])
    return jnp.concatenate([flat, cot, jnp.zeros((5, flat.shape[1]), BF)], 0)


def edge_unpack(packed, bins):
    columns = packed[: 2 * bins].reshape(2, bins, -1)
    cot = packed[2 * bins : 2 * bins + 3].astype(F32).sum(0)
    return columns, cot[None]


def to_spec(forward_tab, block):
    spec = jnp.einsum("jb,pbc->jpc", forward_tab, block, preferred_element_type=F32)
    return spec.astype(BF)


def spectral_tables(modes, bins):
    phase_int = np.arange(modes)[:, None] * np.arange(bins)[None, :] % bins
    angle_val = phase_int.astype(np.float32) * np.float32(2.0 * np.pi / bins)
    cosine = np.cos(angle_val)
    sine = np.sin(angle_val)
    forward_tab = np.concatenate([cosine, -sine], 0)
    weight_k = np.where(np.arange(modes) == 0, 1.0, 2.0).astype(np.float32)[:, None] / bins
    inverse_tab = np.concatenate([cosine * weight_k, -sine * weight_k], 0).T
    tables = np.concatenate([forward_tab, inverse_tab.T], 0)
    return jnp.asarray(tables.astype(jnp.bfloat16))


def gelu_pair(value):
    normal_cdf = 0.5 * (1.0 + jax.scipy.special.erf(value * 0.7071067811865476))
    return (
        value * normal_cdf,
        normal_cdf + value * jnp.exp(-0.5 * value * value) * 0.3989422804014327,
    )


def split3(value):
    top = lax.reduce_precision(value, 8, 7)
    rest = value - top
    mid = lax.reduce_precision(rest, 8, 7)
    return jnp.stack([top, mid, rest - mid], 0).astype(BF)


def exchange(value, axis):
    return lax.all_to_all(value, axis, 0, 0, tiled=True)


def tied(*values):
    return lax.optimization_barrier(values)


def pick_weight(core, got_ref, other_ref, mode, side):
    width = 32
    span = slice(side * width, (side + 1) * width)
    blocks = []
    for part in range(2):
        mine = got_ref[2 * mode + part, span, :]
        other = other_ref[2 * mode + part, span, :]
        blocks.append(jnp.where(core == 0, mine, other))
        blocks.append(jnp.where(core == 0, other, mine))
    return jnp.concatenate(blocks, 0)


def middle_kernel(
    core_ref,
    got_ref,
    other_ref,
    low_ref,
    wide_ref,
    high_ref,
    cot_ref,
    conv_ref,
    table_ref,
    grad_ref,
    sent_ref,
    spec_ref,
    mix_ref,
    turn_ref,
    sum_ref,
):
    modes = table_ref.shape[0] // 4
    forward_tab = table_ref[: 2 * modes, :]
    back = table_ref[2 * modes :, :]
    inverse_tab = back.astype(F32).T.astype(BF)
    near = grad_ref.shape[0]
    cells = near - 2
    bins, chans = grad_ref.shape[1:]
    rows = spec_ref.shape[1]
    band = 32
    core = core_ref[0]
    sum_ref[...] = jnp.zeros_like(sum_ref)
    spec_ref[:, near:, :] = jnp.zeros((2 * modes, rows - near, chans), F32)
    for cell in range(near):
        spec_ref[:, cell, :] = jnp.dot(
            forward_tab, wide_ref[cell + 1], preferred_element_type=F32
        )

    def mix_one(mode, carry):
        lhs = jnp.concatenate([spec_ref[mode], spec_ref[modes + mode]], 0).astype(BF)
        by_real, by_imag = [
            jnp.dot(
                lhs,
                pick_weight(core, got_ref, other_ref, mode, side),
                preferred_element_type=F32,
            )
            for side in range(2)
        ]
        mix_ref[:, mode, :] = by_real[:rows] - by_imag[rows:]
        mix_ref[:, modes + mode, :] = by_imag[:rows] + by_real[rows:]
        return carry

    lax.fori_loop(0, modes, mix_one, 0, unroll=4)

    def one_cell(cell, own):
        spectral = jnp.dot(inverse_tab, mix_ref[cell].astype(BF), preferred_element_type=F32)
        pieces = []
        for start in range(0, bins, band):
            span = slice(start, start + band)
            total = spectral[span]
            windows = []
            for row, ref in enumerate((low_ref, wide_ref, high_ref)):
                for col in range(3):
                    window = ref[cell + col, span, :].astype(F32)
                    windows.append(window)
                    total = total + window * conv_ref[3 * row + col : 3 * row + col + 1, :]
            activ, slope = gelu_pair(total)
            cot = cot_ref[cell, span, :]
            grad = (cot * conv_ref[9:10, :] * slope).astype(BF)
            pieces.append(grad)
            if own:
                wide_grad = grad.astype(F32)
                for index_d, window in enumerate(windows + [None]):
                    term = cot * activ if window is None else window * wide_grad
                    sum_ref[index_d] += jnp.sum(term.reshape(band // 8, 8, chans), 0)
        grad = jnp.concatenate(pieces, 0)
        grad_ref[cell] = grad
        return grad

    one_cell(0, False)
    one_cell(near - 1, False)

    def own_cell(cell, carry):
        grad = one_cell(cell + 1, True)
        turn_ref[:, cell, :] = jnp.dot(back, grad, preferred_element_type=F32)
        return carry

    lax.fori_loop(0, cells, own_cell, 0)
    small = [jnp.sum(sum_ref[index_d], 0, keepdims=True) for index_d in range(10)]
    small = jnp.concatenate(small + [jnp.zeros((6, chans), F32)], 0).astype(BF)

    def pack_one(mode, carry):
        pair = jnp.concatenate([turn_ref[mode], turn_ref[modes + mode]], 0).astype(BF)
        for part in range(2):
            sent_ref[2 * mode + part, 0:16, :] = pair
            sent_ref[2 * mode + part, 16:32, :] = small
        return carry

    lax.fori_loop(0, modes, pack_one, 0, unroll=4)


def last_kernel(
    core_ref,
    got_ref,
    other_ref,
    sent_ref,
    low_ref,
    wide_ref,
    high_ref,
    conv_ref,
    table_ref,
    out_ref,
    stack_ref,
):
    modes = table_ref.shape[0] // 4
    forward_turn = table_ref[: 2 * modes, :].astype(F32).T.astype(BF)
    cells, bins, chans = out_ref.shape
    band = 32
    core = core_ref[0]

    def mix_one(mode, carry):
        lhs = sent_ref[2 * mode, 0:16, :]
        by_real, by_imag = [
            lax.dot_general(
                lhs,
                pick_weight(core, got_ref, other_ref, mode, side),
                (((1,), (1,)), ((), ())),
                preferred_element_type=F32,
            )
            for side in range(2)
        ]
        stack_ref[:, mode, :] = by_real[:cells] + by_imag[cells:]
        stack_ref[:, modes + mode, :] = by_real[cells:] - by_imag[:cells]
        return carry

    lax.fori_loop(0, modes, mix_one, 0, unroll=4)

    def one_cell(cell, carry):
        total = jnp.dot(forward_turn, stack_ref[cell].astype(BF), preferred_element_type=F32)
        for start in range(0, bins, band):
            span = slice(start, start + band)
            part = total[span]
            for row, ref in enumerate((high_ref, wide_ref, low_ref)):
                for col in range(3):
                    window = ref[cell + 2 - col, span, :].astype(F32)
                    part = part + window * conv_ref[3 * row + col : 3 * row + col + 1, :]
            out_ref[cell, span, :] = part
        return carry

    lax.fori_loop(0, cells, one_cell, 0)


def on_core(kernel, operands, out_shape, scratch):
    whole = pl.BlockSpec(memory_space=pltpu.VMEM)
    return pl.pallas_call(
        kernel,
        out_shape=out_shape,
        in_specs=[pl.BlockSpec(memory_space=pltpu.SMEM)] + [whole] * (len(operands) - 1),
        out_specs=jax.tree.map(lambda _: whole, out_shape),
        scratch_shapes=scratch,
        compiler_params=pltpu.CompilerParams(vmem_limit_bytes=20 * 1024 * 1024),
        cost_estimate=pl.CostEstimate(
            flops=200_000_000, bytes_accessed=12_000_000, transcendentals=400_000
        ),
    )(*operands)


def local(hidden, cotangent, spectral_w, conv_k, proj_w):
    rows_here, cols, bins, chans = hidden.shape
    groups = lax.axis_size("grp")
    tiles = lax.axis_size("tile")
    half = spectral_w.shape[0]
    modes = half * tiles // chans
    parts = chans // half
    cells = rows_here * cols
    core = lax.axis_index("grp") % 2
    which = core.astype(jnp.int32).reshape(1)
    quarter = half // 2
    near = cols + 2
    count = conv_k.shape[0] + 1
    tables = spectral_tables(modes, bins)
    gains = jnp.concatenate([conv_k, proj_w[None], jnp.zeros((6, chans), F32)], 0)
    own_rows = lax.dynamic_slice_in_dim(spectral_w, core * quarter, quarter, 0)
    own_rows = jnp.concatenate([own_rows[:, :chans], own_rows[:, chans:]], 0)
    sent = (
        to_spec(tables[: 2 * modes], hidden[0])
        .reshape(2, modes, cells, parts, half)
        .transpose(1, 3, 2, 0, 4)
        .reshape(tiles, cells, 2 * half)
    )
    sent = jnp.concatenate([jnp.broadcast_to(own_rows, (tiles,) + own_rows.shape), sent], 1)
    sent, hidden, cotangent = tied(sent, hidden, cotangent)
    got = exchange(sent, "tile")
    low_t = shifted(edge_pack(hidden[0, cols - 2 :], split3(cotangent[0, cols - 1])), "tile", 1)
    high_t = shifted(edge_pack(hidden[0, :2], split3(cotangent[0, 0])), "tile", -1)
    got, low_t, high_t = tied(got, low_t, high_t)
    low_cols, low_cot = edge_unpack(low_t, bins)
    high_cols, high_cot = edge_unpack(high_t, bins)
    wide = jnp.concatenate([low_cols, hidden[0], high_cols], 0)
    cot_wide = jnp.concatenate([low_cot, cotangent[0], high_cot], 0)
    cot_lanes = jnp.broadcast_to(cot_wide[:, :, None], (near, bins, chans))
    low_g = shifted(wide, "grp", 1)
    high_g = shifted(wide, "grp", -1)
    swap = [(i, i ^ 1) for i in range(groups)]
    other = lax.ppermute(got, "grp", swap)
    grad_wide, grad_sent = on_core(
        middle_kernel,
        (
            which,
            got,
            other,
            low_g,
            wide,
            high_g,
            cot_lanes,
            gains,
            tables,
        ),
        (
            jax.ShapeDtypeStruct((near, bins, chans), BF),
            jax.ShapeDtypeStruct((tiles, 32, chans), BF),
        ),
        [
            pltpu.VMEM((2 * modes, 16, chans), F32),
            pltpu.VMEM((16, 2 * modes, chans), F32),
            pltpu.VMEM((2 * modes, cells, chans), F32),
            pltpu.VMEM((count, 8, chans), F32),
        ],
    )
    low_gg = shifted(grad_wide, "grp", 1)
    high_gg = shifted(grad_wide, "grp", -1)
    got_g = exchange(grad_sent, "tile")
    own_h, _ = tied(got[:, 2 * quarter :], grad_sent)
    got_g, low_gg, high_gg = tied(got_g, low_gg, high_gg)
    lane = lax.broadcasted_iota(jnp.int32, own_h.shape, 2)
    left = jnp.concatenate([jnp.where(lane < half, own_h, -own_h), jnp.roll(own_h, half, 2)], 1)
    weight_part = lax.dot_general(
        left.reshape(tiles * 2 * cells, 2 * half),
        got_g[:, : 2 * cells].reshape(tiles * 2 * cells, chans),
        (((0,), (0,)), ((), ())),
        preferred_element_type=F32,
    ).astype(BF)
    totals = jnp.sum(got_g[:, 2 * cells : 2 * cells + count].astype(F32), 0)
    totals = split3(totals).reshape(3 * count, chans)
    grad_hidden = on_core(
        last_kernel,
        (
            which,
            got,
            other,
            grad_sent,
            low_gg,
            grad_wide,
            high_gg,
            gains,
            tables,
        ),
        jax.ShapeDtypeStruct((cells, bins, chans), F32),
        [pltpu.VMEM((cells, 2 * modes, chans), F32)],
    ).reshape(rows_here, cols, bins, chans)
    last = jnp.concatenate([weight_part, totals], 0)
    last = exchange(jnp.broadcast_to(last, (groups,) + last.shape), "grp")
    grad_spectral = jnp.sum(last[:, : 2 * half].astype(F32), 0)
    grad_spectral = jnp.concatenate([grad_spectral[:half], grad_spectral[half:]], 1)
    totals = last[:, 2 * half :].astype(F32).reshape(groups, 3, count, chans)
    totals = jnp.sum(totals, (0, 1))
    return (grad_hidden, grad_spectral, totals[: count - 1], totals[count - 1])


def solution(mesh):
    in_specs = (P("grp", "tile", None, None), P("grp", "tile", None), P("tile", None), P(), P())
    out_specs = (P("grp", "tile", None, None), P("tile", None), P(), P())
    return jax.shard_map(local, mesh=mesh, in_specs=in_specs, out_specs=out_specs, check_vma=False)
```

```python
import jax
import jax.numpy as jnp
import numpy as np
from jax import lax
from jax.experimental import pallas as pl
from jax.experimental.pallas import tpu as pltpu
from jax.sharding import PartitionSpec as P

BF = jnp.bfloat16
F32 = jnp.float32


def shifted(block, axis, step):
    count = lax.axis_size(axis)
    pairs = [(i, i + step) for i in range(count) if 0 <= i + step < count]
    return lax.ppermute(block, axis, pairs)


def mate(block):
    return lax.ppermute(block, "grp", [(i, i ^ 1) for i in range(lax.axis_size("grp"))])


def across(block, step):
    rows, cols = lax.axis_size("grp"), lax.axis_size("tile")
    pairs = []
    for row in range(rows):
        far = row + 1 if row % 2 else row - 1
        if 0 <= far < rows:
            pairs += [
                (row * cols + col, far * cols + col + step)
                for col in range(cols)
                if 0 <= col + step < cols
            ]
    return lax.ppermute(block, ("grp", "tile"), pairs)


def edge_pack(columns, cot):
    flat = columns.reshape(-1, columns.shape[-1])
    return jnp.concatenate([flat, cot, jnp.zeros((5, flat.shape[1]), BF)], 0)


def edge_unpack(packed, bins):
    columns = packed[: 2 * bins].reshape(2, bins, -1)
    cot = packed[2 * bins : 2 * bins + 3].astype(F32).sum(0)
    return columns, cot[None]


def to_spec(forward_tab, block):
    spec = jnp.einsum("jb,pbc->jpc", forward_tab, block, preferred_element_type=F32)
    return spec.astype(BF)


def spectral_tables(modes, bins):
    phase_int = np.arange(modes)[:, None] * np.arange(bins)[None, :] % bins
    angle_val = phase_int.astype(np.float32) * np.float32(2.0 * np.pi / bins)
    cosine = np.cos(angle_val)
    sine = np.sin(angle_val)
    forward_tab = np.concatenate([cosine, -sine], 0)
    weight_k = np.where(np.arange(modes) == 0, 1.0, 2.0).astype(np.float32)[:, None] / bins
    inverse_tab = np.concatenate([cosine * weight_k, -sine * weight_k], 0).T
    tables = np.concatenate([forward_tab, inverse_tab.T], 0)
    return jnp.asarray(tables.astype(jnp.bfloat16))


def gelu_pair(value):
    normal_cdf = 0.5 * (1.0 + jax.scipy.special.erf(value * 0.7071067811865476))
    return (
        value * normal_cdf,
        normal_cdf + value * jnp.exp(-0.5 * value * value) * 0.3989422804014327,
    )


def split3(value):
    top = lax.reduce_precision(value, 8, 7)
    rest = value - top
    mid = lax.reduce_precision(rest, 8, 7)
    return jnp.stack([top, mid, rest - mid], 0).astype(BF)


def exchange(value, axis):
    return lax.all_to_all(value, axis, 0, 0, tiled=True)


def tied(*values):
    return lax.optimization_barrier(values)


def pick_weight(core, got_ref, other_ref, mode, side):
    width = 32
    span = slice(side * width, (side + 1) * width)
    blocks = []
    for part in range(2):
        mine = got_ref[2 * mode + part, span, :]
        other = other_ref[2 * mode + part, span, :]
        blocks.append(jnp.where(core == 0, mine, other))
        blocks.append(jnp.where(core == 0, other, mine))
    return jnp.concatenate(blocks, 0)


def middle_kernel(
    core_ref,
    got_ref,
    other_ref,
    far_ref,
    wide_ref,
    close_ref,
    cot_ref,
    conv_ref,
    table_ref,
    grad_ref,
    sent_ref,
    spec_ref,
    mix_ref,
    turn_ref,
    sum_ref,
):
    modes = table_ref.shape[0] // 4
    forward_tab = table_ref[: 2 * modes, :]
    back = table_ref[2 * modes :, :]
    inverse_tab = back.astype(F32).T.astype(BF)
    near = grad_ref.shape[0]
    cells = near - 2
    bins, chans = grad_ref.shape[1:]
    rows = spec_ref.shape[1]
    band = 32
    core = core_ref[0]
    sum_ref[...] = jnp.zeros_like(sum_ref)
    spec_ref[:, near:, :] = jnp.zeros((2 * modes, rows - near, chans), F32)
    for cell in range(near):
        spec_ref[:, cell, :] = jnp.dot(
            forward_tab, wide_ref[cell + 1], preferred_element_type=F32
        )

    def mix_one(mode, carry):
        lhs = jnp.concatenate([spec_ref[mode], spec_ref[modes + mode]], 0).astype(BF)
        by_real, by_imag = [
            jnp.dot(
                lhs,
                pick_weight(core, got_ref, other_ref, mode, side),
                preferred_element_type=F32,
            )
            for side in range(2)
        ]
        mix_ref[:, mode, :] = by_real[:rows] - by_imag[rows:]
        mix_ref[:, modes + mode, :] = by_imag[:rows] + by_real[rows:]
        return carry

    lax.fori_loop(0, modes, mix_one, 0, unroll=4)

    def one_cell(cell, own):
        spectral = jnp.dot(inverse_tab, mix_ref[cell].astype(BF), preferred_element_type=F32)
        pieces = []
        for start in range(0, bins, band):
            span = slice(start, start + band)
            total = spectral[span]
            windows = []
            for row, ref in enumerate((far_ref, wide_ref, close_ref)):
                for col in range(3):
                    window = ref[cell + col, span, :].astype(F32)
                    windows.append(window)
                    total = total + window * conv_ref[3 * row + col : 3 * row + col + 1, :]
            activ, slope = gelu_pair(total)
            cot = cot_ref[cell, span, :]
            grad = (cot * conv_ref[9:10, :] * slope).astype(BF)
            pieces.append(grad)
            if own:
                wide_grad = grad.astype(F32)
                for index_d, window in enumerate(windows + [None]):
                    term = cot * activ if window is None else window * wide_grad
                    sum_ref[index_d] += jnp.sum(term.reshape(band // 8, 8, chans), 0)
        grad = jnp.concatenate(pieces, 0)
        grad_ref[cell] = grad
        return grad

    one_cell(0, False)
    one_cell(near - 1, False)

    def own_cell(cell, carry):
        grad = one_cell(cell + 1, True)
        turn_ref[:, cell, :] = jnp.dot(back, grad, preferred_element_type=F32)
        return carry

    lax.fori_loop(0, cells, own_cell, 0)
    small = [jnp.sum(sum_ref[index_d], 0, keepdims=True) for index_d in range(10)]
    upper, lower = jnp.concatenate(small[:3], 0), jnp.concatenate(small[6:9], 0)
    small = jnp.concatenate(
        [
            jnp.where(core == 0, upper, lower),
            *small[3:6],
            jnp.where(core == 0, lower, upper),
            small[9],
            jnp.zeros((6, chans), F32),
        ],
        0,
    ).astype(BF)

    def pack_one(mode, carry):
        pair = jnp.concatenate([turn_ref[mode], turn_ref[modes + mode]], 0).astype(BF)
        for part in range(2):
            sent_ref[2 * mode + part, 0:16, :] = pair
            sent_ref[2 * mode + part, 16:32, :] = small
        return carry

    lax.fori_loop(0, modes, pack_one, 0, unroll=4)


def last_kernel(
    core_ref,
    got_ref,
    other_ref,
    sent_ref,
    far_ref,
    wide_ref,
    close_ref,
    conv_ref,
    table_ref,
    out_ref,
    stack_ref,
):
    modes = table_ref.shape[0] // 4
    forward_turn = table_ref[: 2 * modes, :].astype(F32).T.astype(BF)
    cells, bins, chans = out_ref.shape
    band = 32
    core = core_ref[0]

    def mix_one(mode, carry):
        lhs = sent_ref[2 * mode, 0:16, :]
        by_real, by_imag = [
            lax.dot_general(
                lhs,
                pick_weight(core, got_ref, other_ref, mode, side),
                (((1,), (1,)), ((), ())),
                preferred_element_type=F32,
            )
            for side in range(2)
        ]
        stack_ref[:, mode, :] = by_real[:cells] + by_imag[cells:]
        stack_ref[:, modes + mode, :] = by_real[cells:] - by_imag[:cells]
        return carry

    lax.fori_loop(0, modes, mix_one, 0, unroll=4)

    def one_cell(cell, carry):
        total = jnp.dot(forward_turn, stack_ref[cell].astype(BF), preferred_element_type=F32)
        for start in range(0, bins, band):
            span = slice(start, start + band)
            part = total[span]
            for row, ref in enumerate((close_ref, wide_ref, far_ref)):
                for col in range(3):
                    window = ref[cell + 2 - col, span, :].astype(F32)
                    part = part + window * conv_ref[3 * row + col : 3 * row + col + 1, :]
            out_ref[cell, span, :] = part
        return carry

    lax.fori_loop(0, cells, one_cell, 0)


def gather_kernel(left_ref, got_ref, out_ref):
    tiles, rows, width = left_ref.shape
    chans = got_ref.shape[2]
    term = lax.dot_general(
        left_ref[...].reshape(tiles * rows, width),
        got_ref[:, :rows, :].reshape(tiles * rows, chans),
        (((0,), (0,)), ((), ())),
        preferred_element_type=F32,
    ).astype(BF)
    total = jnp.sum(got_ref[:, rows:, :].astype(F32), 0)
    pieces = [term]
    for _ in range(3):
        piece = total.astype(BF)
        total = total - piece.astype(F32)
        pieces.append(piece)
    block = jnp.concatenate(pieces, 0)
    for group in range(out_ref.shape[0]):
        out_ref[group] = block


def finish_kernel(last_ref, spectral_ref, conv_ref, proj_ref):
    half, width = spectral_ref.shape
    total = jnp.sum(last_ref[...].astype(F32), 0)
    spectral_ref[:, : width // 2] = total[:half]
    spectral_ref[:, width // 2 :] = total[half : 2 * half]
    rest = total[2 * half :]
    rest = rest[:16] + rest[16:32] + rest[32:]
    conv_ref[...] = rest[:9]
    proj_ref[...] = rest[9:10]


def on_core(kernel, operands, out_shape, scratch=(), scalars=1):
    whole = pl.BlockSpec(memory_space=pltpu.VMEM)
    return pl.pallas_call(
        kernel,
        out_shape=out_shape,
        in_specs=[pl.BlockSpec(memory_space=pltpu.SMEM)] * scalars
        + [whole] * (len(operands) - scalars),
        out_specs=jax.tree.map(lambda _: whole, out_shape),
        scratch_shapes=scratch,
        compiler_params=pltpu.CompilerParams(vmem_limit_bytes=20 * 1024 * 1024),
        cost_estimate=pl.CostEstimate(
            flops=200_000_000, bytes_accessed=12_000_000, transcendentals=400_000
        ),
    )(*operands)


def local(hidden, cotangent, spectral_w, conv_k, proj_w):
    rows_here, cols, bins, chans = hidden.shape
    groups = lax.axis_size("grp")
    tiles = lax.axis_size("tile")
    half = spectral_w.shape[0]
    modes = half * tiles // chans
    parts = chans // half
    cells = rows_here * cols
    core = lax.axis_index("grp") % 2
    which = core.astype(jnp.int32).reshape(1)
    quarter = half // 2
    near = cols + 2
    count = conv_k.shape[0] + 1
    tables = spectral_tables(modes, bins)
    upper, centre, lower = conv_k[:3], conv_k[3:6], conv_k[6:]
    gains = jnp.concatenate(
        [
            jnp.where(core == 0, upper, lower),
            centre,
            jnp.where(core == 0, lower, upper),
            proj_w[None],
            jnp.zeros((6, chans), F32),
        ],
        0,
    )
    own_rows = lax.dynamic_slice_in_dim(spectral_w, core * quarter, quarter, 0)
    own_rows = jnp.concatenate([own_rows[:, :chans], own_rows[:, chans:]], 0)
    sent = (
        to_spec(tables[: 2 * modes], hidden[0])
        .reshape(2, modes, cells, parts, half)
        .transpose(1, 3, 2, 0, 4)
        .reshape(tiles, cells, 2 * half)
    )
    sent = jnp.concatenate([jnp.broadcast_to(own_rows, (tiles,) + own_rows.shape), sent], 1)
    sent, hidden, cotangent = tied(sent, hidden, cotangent)
    got = exchange(sent, "tile")
    head, tail = hidden[0, :2], hidden[0, cols - 2 :]
    low_t = shifted(edge_pack(tail, split3(cotangent[0, cols - 1])), "tile", 1)
    high_t = shifted(edge_pack(head, split3(cotangent[0, 0])), "tile", -1)
    far = [across(tail, 1), across(hidden[0], 0), across(head, -1)]
    got, low_t, high_t, far = tied(got, low_t, high_t, far)
    far = jnp.concatenate(far, 0)
    low_cols, low_cot = edge_unpack(low_t, bins)
    high_cols, high_cot = edge_unpack(high_t, bins)
    wide = jnp.concatenate([low_cols, hidden[0], high_cols], 0)
    cot_wide = jnp.concatenate([low_cot, cotangent[0], high_cot], 0)
    cot_lanes = jnp.broadcast_to(cot_wide[:, :, None], (near, bins, chans))
    other = mate(got)
    close = mate(wide)
    grad_wide, grad_sent = on_core(
        middle_kernel,
        (
            which,
            got,
            other,
            far,
            wide,
            close,
            cot_lanes,
            gains,
            tables,
        ),
        (
            jax.ShapeDtypeStruct((near, bins, chans), BF),
            jax.ShapeDtypeStruct((tiles, 32, chans), BF),
        ),
        [
            pltpu.VMEM((2 * modes, 16, chans), F32),
            pltpu.VMEM((16, 2 * modes, chans), F32),
            pltpu.VMEM((2 * modes, cells, chans), F32),
            pltpu.VMEM((count, 8, chans), F32),
        ],
    )
    far_grad = across(grad_wide, 0)
    close_grad = mate(grad_wide)
    got_g = exchange(grad_sent, "tile")
    late, _ = tied(got, grad_sent)
    own_h = late[:, 2 * quarter :]
    got_g, far_grad, close_grad = tied(got_g, far_grad, close_grad)
    lane = lax.broadcasted_iota(jnp.int32, own_h.shape, 2)
    left = jnp.concatenate([jnp.where(lane < half, own_h, -own_h), jnp.roll(own_h, half, 2)], 1)
    last = on_core(
        gather_kernel,
        (left, got_g),
        jax.ShapeDtypeStruct((groups, 2 * half + 48, chans), BF),
        scalars=0,
    )
    grad_hidden = on_core(
        last_kernel,
        (
            which,
            got,
            other,
            grad_sent,
            far_grad,
            grad_wide,
            close_grad,
            gains,
            tables,
        ),
        jax.ShapeDtypeStruct((cells, bins, chans), F32),
        [pltpu.VMEM((cells, 2 * modes, chans), F32)],
    ).reshape(rows_here, cols, bins, chans)
    grad_spectral, grad_conv, grad_proj = on_core(
        finish_kernel,
        (exchange(last, "grp"),),
        (
            jax.ShapeDtypeStruct((half, 2 * chans), F32),
            jax.ShapeDtypeStruct((count - 1, chans), F32),
            jax.ShapeDtypeStruct((1, chans), F32),
        ),
        scalars=0,
    )
    return (grad_hidden, grad_spectral, grad_conv, grad_proj[0])


def solution(mesh):
    in_specs = (P("grp", "tile", None, None), P("grp", "tile", None), P("tile", None), P(), P())
    out_specs = (P("grp", "tile", None, None), P("tile", None), P(), P())
    return jax.shard_map(local, mesh=mesh, in_specs=in_specs, out_specs=out_specs, check_vma=False)
```

```python
import jax
import jax.numpy as jnp
import numpy as np
from jax import lax
from jax.experimental import pallas as pl
from jax.experimental.pallas import tpu as pltpu
from jax.sharding import PartitionSpec as P

BF = jnp.bfloat16
F32 = jnp.float32


def shifted(block, axis, step):
    count = lax.axis_size(axis)
    pairs = [(i, i + step) for i in range(count) if 0 <= i + step < count]
    return lax.ppermute(block, axis, pairs)


def mate(block):
    return lax.ppermute(block, "grp", [(i, i ^ 1) for i in range(lax.axis_size("grp"))])


def across(block, step):
    rows, cols = lax.axis_size("grp"), lax.axis_size("tile")
    pairs = []
    for row in range(rows):
        far = row + 1 if row % 2 else row - 1
        if 0 <= far < rows:
            pairs += [
                (row * cols + col, far * cols + col + step)
                for col in range(cols)
                if 0 <= col + step < cols
            ]
    return lax.ppermute(block, ("grp", "tile"), pairs)


def edge_pack(columns, cot):
    bins = columns.shape[1]
    extra = jnp.pad(cot, ((0, bins - cot.shape[0]), (0, 0)))
    return jnp.concatenate([columns, extra[None]], 0)


def edge_unpack(packed):
    cot = packed[2, :3].astype(F32).sum(0)
    return packed[:2], cot[None]


def to_spec(forward_tab, block):
    spec = jnp.einsum("jb,pbc->jpc", forward_tab, block, preferred_element_type=F32)
    return spec.astype(BF)


def spectral_tables(modes, bins):
    phase_int = np.arange(modes)[:, None] * np.arange(bins)[None, :] % bins
    angle_val = phase_int.astype(np.float32) * np.float32(2.0 * np.pi / bins)
    cosine = np.cos(angle_val)
    sine = np.sin(angle_val)
    forward_tab = np.concatenate([cosine, -sine], 0)
    weight_k = np.where(np.arange(modes) == 0, 1.0, 2.0).astype(np.float32)[:, None] / bins
    inverse_tab = np.concatenate([cosine * weight_k, -sine * weight_k], 0).T
    tables = np.concatenate([forward_tab, inverse_tab.T], 0)
    return jnp.asarray(tables.astype(jnp.bfloat16))


def gelu_pair(value):
    normal_cdf = 0.5 * (1.0 + jax.scipy.special.erf(value * 0.7071067811865476))
    return (
        value * normal_cdf,
        normal_cdf + value * jnp.exp(-0.5 * value * value) * 0.3989422804014327,
    )


def split3(value):
    top = lax.reduce_precision(value, 8, 7)
    rest = value - top
    mid = lax.reduce_precision(rest, 8, 7)
    return jnp.stack([top, mid, rest - mid], 0).astype(BF)


def exchange(value, axis):
    return lax.all_to_all(value, axis, 0, 0, tiled=True)


def tied(*values):
    return lax.optimization_barrier(values)


def pick_weight(core, got_ref, other_ref, mode, side):
    width = 32
    span = slice(side * width, (side + 1) * width)
    blocks = []
    for part in range(2):
        mine = got_ref[2 * mode + part, span, :]
        other = other_ref[2 * mode + part, span, :]
        blocks.append(jnp.where(core == 0, mine, other))
        blocks.append(jnp.where(core == 0, other, mine))
    return jnp.concatenate(blocks, 0)


def middle_kernel(
    core_ref,
    got_ref,
    other_ref,
    far_ref,
    wide_ref,
    close_ref,
    cot_ref,
    conv_ref,
    table_ref,
    grad_ref,
    sent_ref,
    spec_ref,
    mix_ref,
    turn_ref,
    sum_ref,
):
    modes = table_ref.shape[0] // 4
    forward_tab = table_ref[: 2 * modes, :]
    back = table_ref[2 * modes :, :]
    inverse_tab = back.astype(F32).T.astype(BF)
    near = grad_ref.shape[0]
    cells = near - 2
    bins, chans = grad_ref.shape[1:]
    rows = spec_ref.shape[1]
    band = 32
    core = core_ref[0]
    sum_ref[...] = jnp.zeros_like(sum_ref)
    spec_ref[:, near:, :] = jnp.zeros((2 * modes, rows - near, chans), F32)
    for cell in range(near):
        spec_ref[:, cell, :] = jnp.dot(
            forward_tab, wide_ref[cell + 1], preferred_element_type=F32
        )

    def mix_one(mode, carry):
        lhs = jnp.concatenate([spec_ref[mode], spec_ref[modes + mode]], 0).astype(BF)
        by_real, by_imag = [
            jnp.dot(
                lhs,
                pick_weight(core, got_ref, other_ref, mode, side),
                preferred_element_type=F32,
            )
            for side in range(2)
        ]
        mix_ref[:, mode, :] = by_real[:rows] - by_imag[rows:]
        mix_ref[:, modes + mode, :] = by_imag[:rows] + by_real[rows:]
        return carry

    lax.fori_loop(0, modes, mix_one, 0, unroll=4)

    def one_cell(cell, own):
        spectral = jnp.dot(inverse_tab, mix_ref[cell].astype(BF), preferred_element_type=F32)
        pieces = []
        for start in range(0, bins, band):
            span = slice(start, start + band)
            total = spectral[span]
            windows = []
            for row, ref in enumerate((far_ref, wide_ref, close_ref)):
                for col in range(3):
                    window = ref[cell + col, span, :].astype(F32)
                    windows.append(window)
                    total = total + window * conv_ref[3 * row + col : 3 * row + col + 1, :]
            activ, slope = gelu_pair(total)
            cot = cot_ref[cell, span, :]
            grad = (cot * conv_ref[9:10, :] * slope).astype(BF)
            pieces.append(grad)
            if own:
                wide_grad = grad.astype(F32)
                for index_d, window in enumerate(windows + [None]):
                    term = cot * activ if window is None else window * wide_grad
                    sum_ref[index_d] += jnp.sum(term.reshape(band // 8, 8, chans), 0)
        grad = jnp.concatenate(pieces, 0)
        grad_ref[cell] = grad
        return grad

    one_cell(0, False)
    one_cell(near - 1, False)

    def own_cell(cell, carry):
        grad = one_cell(cell + 1, True)
        turn_ref[:, cell, :] = jnp.dot(back, grad, preferred_element_type=F32)
        return carry

    lax.fori_loop(0, cells, own_cell, 0)
    small = [jnp.sum(sum_ref[index_d], 0, keepdims=True) for index_d in range(10)]
    upper, lower = jnp.concatenate(small[:3], 0), jnp.concatenate(small[6:9], 0)
    small = jnp.concatenate(
        [
            jnp.where(core == 0, upper, lower),
            *small[3:6],
            jnp.where(core == 0, lower, upper),
            small[9],
            jnp.zeros((6, chans), F32),
        ],
        0,
    ).astype(BF)

    def pack_one(mode, carry):
        pair = jnp.concatenate([turn_ref[mode], turn_ref[modes + mode]], 0).astype(BF)
        for part in range(2):
            sent_ref[2 * mode + part, 0:16, :] = pair
            sent_ref[2 * mode + part, 16:32, :] = small
        return carry

    lax.fori_loop(0, modes, pack_one, 0, unroll=4)


def last_kernel(
    core_ref,
    got_ref,
    other_ref,
    sent_ref,
    far_ref,
    wide_ref,
    close_ref,
    conv_ref,
    table_ref,
    out_ref,
    stack_ref,
):
    modes = table_ref.shape[0] // 4
    forward_turn = table_ref[: 2 * modes, :].astype(F32).T.astype(BF)
    cells, bins, chans = out_ref.shape
    band = 32
    core = core_ref[0]

    def mix_one(mode, carry):
        lhs = sent_ref[2 * mode, 0:16, :]
        by_real, by_imag = [
            lax.dot_general(
                lhs,
                pick_weight(core, got_ref, other_ref, mode, side),
                (((1,), (1,)), ((), ())),
                preferred_element_type=F32,
            )
            for side in range(2)
        ]
        stack_ref[:, mode, :] = by_real[:cells] + by_imag[cells:]
        stack_ref[:, modes + mode, :] = by_real[cells:] - by_imag[:cells]
        return carry

    lax.fori_loop(0, modes, mix_one, 0, unroll=4)

    def one_cell(cell, carry):
        total = jnp.dot(forward_turn, stack_ref[cell].astype(BF), preferred_element_type=F32)
        for start in range(0, bins, band):
            span = slice(start, start + band)
            part = total[span]
            for row, ref in enumerate((close_ref, wide_ref, far_ref)):
                for col in range(3):
                    window = ref[cell + 2 - col, span, :].astype(F32)
                    part = part + window * conv_ref[3 * row + col : 3 * row + col + 1, :]
            out_ref[cell, span, :] = part
        return carry

    lax.fori_loop(0, cells, one_cell, 0)


def gather_kernel(left_ref, got_ref, out_ref):
    tiles, rows, width = left_ref.shape
    chans = got_ref.shape[2]
    term = lax.dot_general(
        left_ref[...].reshape(tiles * rows, width),
        got_ref[:, :rows, :].reshape(tiles * rows, chans),
        (((0,), (0,)), ((), ())),
        preferred_element_type=F32,
    ).astype(BF)
    total = jnp.sum(got_ref[:, rows:, :].astype(F32), 0)
    pieces = [term]
    for _ in range(3):
        piece = total.astype(BF)
        total = total - piece.astype(F32)
        pieces.append(piece)
    block = jnp.concatenate(pieces, 0)
    for group in range(out_ref.shape[0]):
        out_ref[group] = block


def finish_kernel(last_ref, spectral_ref, conv_ref, proj_ref):
    half, width = spectral_ref.shape
    total = jnp.sum(last_ref[...].astype(F32), 0)
    spectral_ref[:, : width // 2] = total[:half]
    spectral_ref[:, width // 2 :] = total[half : 2 * half]
    rest = total[2 * half :]
    rest = rest[:16] + rest[16:32] + rest[32:]
    conv_ref[...] = rest[:9]
    proj_ref[...] = rest[9:10]


def on_core(kernel, operands, out_shape, scratch=(), scalars=1):
    whole = pl.BlockSpec(memory_space=pltpu.VMEM)
    return pl.pallas_call(
        kernel,
        out_shape=out_shape,
        in_specs=[pl.BlockSpec(memory_space=pltpu.SMEM)] * scalars
        + [whole] * (len(operands) - scalars),
        out_specs=jax.tree.map(lambda _: whole, out_shape),
        scratch_shapes=scratch,
        compiler_params=pltpu.CompilerParams(vmem_limit_bytes=20 * 1024 * 1024),
        cost_estimate=pl.CostEstimate(
            flops=200_000_000, bytes_accessed=12_000_000, transcendentals=400_000
        ),
    )(*operands)


def local(hidden, cotangent, spectral_w, conv_k, proj_w):
    rows_here, cols, bins, chans = hidden.shape
    groups = lax.axis_size("grp")
    tiles = lax.axis_size("tile")
    half = spectral_w.shape[0]
    modes = half * tiles // chans
    parts = chans // half
    cells = rows_here * cols
    core = lax.axis_index("grp") % 2
    which = core.astype(jnp.int32).reshape(1)
    quarter = half // 2
    near = cols + 2
    count = conv_k.shape[0] + 1
    tables = spectral_tables(modes, bins)
    upper, centre, lower = conv_k[:3], conv_k[3:6], conv_k[6:]
    gains = jnp.concatenate(
        [
            jnp.where(core == 0, upper, lower),
            centre,
            jnp.where(core == 0, lower, upper),
            proj_w[None],
            jnp.zeros((6, chans), F32),
        ],
        0,
    )
    own_rows = lax.dynamic_slice_in_dim(spectral_w, core * quarter, quarter, 0)
    own_rows = jnp.concatenate([own_rows[:, :chans], own_rows[:, chans:]], 0)
    sent = (
        to_spec(tables[: 2 * modes], hidden[0])
        .reshape(2, modes, cells, parts, half)
        .transpose(1, 3, 2, 0, 4)
        .reshape(tiles, cells, 2 * half)
    )
    sent = jnp.concatenate([jnp.broadcast_to(own_rows, (tiles,) + own_rows.shape), sent], 1)
    sent, hidden, cotangent = tied(sent, hidden, cotangent)
    got = exchange(sent, "tile")
    head, tail = hidden[0, :2], hidden[0, cols - 2 :]
    low_t = shifted(edge_pack(tail, split3(cotangent[0, cols - 1])), "tile", 1)
    high_t = shifted(edge_pack(head, split3(cotangent[0, 0])), "tile", -1)
    far = [across(tail, 1), across(hidden[0], 0), across(head, -1)]
    got, low_t, high_t, far = tied(got, low_t, high_t, far)
    far = jnp.concatenate(far, 0)
    low_cols, low_cot = edge_unpack(low_t)
    high_cols, high_cot = edge_unpack(high_t)
    wide = jnp.concatenate([low_cols, hidden[0], high_cols], 0)
    cot_wide = jnp.concatenate([low_cot, cotangent[0], high_cot], 0)
    cot_lanes = jnp.broadcast_to(cot_wide[:, :, None], (near, bins, chans))
    other = mate(got)
    close = mate(wide)
    grad_wide, grad_sent = on_core(
        middle_kernel,
        (
            which,
            got,
            other,
            far,
            wide,
            close,
            cot_lanes,
            gains,
            tables,
        ),
        (
            jax.ShapeDtypeStruct((near, bins, chans), BF),
            jax.ShapeDtypeStruct((tiles, 32, chans), BF),
        ),
        [
            pltpu.VMEM((2 * modes, 16, chans), F32),
            pltpu.VMEM((16, 2 * modes, chans), F32),
            pltpu.VMEM((2 * modes, cells, chans), F32),
            pltpu.VMEM((count, 8, chans), F32),
        ],
    )
    far_grad = across(grad_wide, 0)
    close_grad = mate(grad_wide)
    got_g = exchange(grad_sent, "tile")
    late, _ = tied(got, grad_sent)
    own_h = late[:, 2 * quarter :]
    got_g, far_grad, close_grad = tied(got_g, far_grad, close_grad)
    lane = lax.broadcasted_iota(jnp.int32, own_h.shape, 2)
    left = jnp.concatenate([jnp.where(lane < half, own_h, -own_h), jnp.roll(own_h, half, 2)], 1)
    last = on_core(
        gather_kernel,
        (left, got_g),
        jax.ShapeDtypeStruct((groups, 2 * half + 48, chans), BF),
        scalars=0,
    )
    grad_hidden = on_core(
        last_kernel,
        (
            which,
            got,
            other,
            grad_sent,
            far_grad,
            grad_wide,
            close_grad,
            gains,
            tables,
        ),
        jax.ShapeDtypeStruct((cells, bins, chans), F32),
        [pltpu.VMEM((cells, 2 * modes, chans), F32)],
    ).reshape(rows_here, cols, bins, chans)
    grad_spectral, grad_conv, grad_proj = on_core(
        finish_kernel,
        (exchange(last, "grp"),),
        (
            jax.ShapeDtypeStruct((half, 2 * chans), F32),
            jax.ShapeDtypeStruct((count - 1, chans), F32),
            jax.ShapeDtypeStruct((1, chans), F32),
        ),
        scalars=0,
    )
    return (grad_hidden, grad_spectral, grad_conv, grad_proj[0])


def solution(mesh):
    in_specs = (P("grp", "tile", None, None), P("grp", "tile", None), P("tile", None), P(), P())
    out_specs = (P("grp", "tile", None, None), P("tile", None), P(), P())
    return jax.shard_map(local, mesh=mesh, in_specs=in_specs, out_specs=out_specs, check_vma=False)
```

```python
import jax
import jax.numpy as jnp
import numpy as np
from jax import lax
from jax.experimental import pallas as pl
from jax.experimental.pallas import tpu as pltpu
from jax.sharding import PartitionSpec as P

BF = jnp.bfloat16
F32 = jnp.float32


def shifted(block, axis, step):
    count = lax.axis_size(axis)
    pairs = [(i, i + step) for i in range(count) if 0 <= i + step < count]
    return lax.ppermute(block, axis, pairs)


def mate(block):
    return lax.ppermute(block, "grp", [(i, i ^ 1) for i in range(lax.axis_size("grp"))])


def across(block, step):
    rows, cols = lax.axis_size("grp"), lax.axis_size("tile")
    pairs = []
    for row in range(rows):
        far = row + 1 if row % 2 else row - 1
        if 0 <= far < rows:
            pairs += [
                (row * cols + col, far * cols + col + step)
                for col in range(cols)
                if 0 <= col + step < cols
            ]
    return lax.ppermute(block, ("grp", "tile"), pairs)


def edge_pack(cot, bins):
    return jnp.pad(cot, ((0, bins - cot.shape[0]), (0, 0)))[None]


def to_spec(forward_tab, block):
    spec = jnp.einsum("jb,pbc->jpc", forward_tab, block, preferred_element_type=F32)
    return spec.astype(BF)


def spectral_tables(modes, bins):
    phase_int = np.arange(modes)[:, None] * np.arange(bins)[None, :] % bins
    angle_val = phase_int.astype(np.float32) * np.float32(2.0 * np.pi / bins)
    cosine = np.cos(angle_val)
    sine = np.sin(angle_val)
    forward_tab = np.concatenate([cosine, -sine], 0)
    weight_k = np.where(np.arange(modes) == 0, 1.0, 2.0).astype(np.float32)[:, None] / bins
    inverse_tab = np.concatenate([cosine * weight_k, -sine * weight_k], 0).T
    tables = np.concatenate([forward_tab, inverse_tab.T], 0)
    return jnp.asarray(tables.astype(jnp.bfloat16))


def gelu_pair(value):
    normal_cdf = 0.5 * (1.0 + jax.scipy.special.erf(value * 0.7071067811865476))
    return (
        value * normal_cdf,
        normal_cdf + value * jnp.exp(-0.5 * value * value) * 0.3989422804014327,
    )


def split3(value):
    top = lax.reduce_precision(value, 8, 7)
    rest = value - top
    mid = lax.reduce_precision(rest, 8, 7)
    return jnp.stack([top, mid, rest - mid], 0).astype(BF)


def exchange(value, axis):
    return lax.all_to_all(value, axis, 0, 0, tiled=True)


def tied(*values):
    return lax.optimization_barrier(values)


def pick_weight(core, got_ref, other_ref, mode, side):
    width = 32
    span = slice(side * width, (side + 1) * width)
    blocks = []
    for part in range(2):
        mine = got_ref[2 * mode + part, span, :]
        other = other_ref[2 * mode + part, span, :]
        blocks.append(jnp.where(core == 0, mine, other))
        blocks.append(jnp.where(core == 0, other, mine))
    return jnp.concatenate(blocks, 0)


def middle_kernel(
    core_ref,
    got_ref,
    other_ref,
    far_ref,
    wide_ref,
    close_ref,
    cot_ref,
    conv_ref,
    table_ref,
    grad_ref,
    sent_ref,
    spec_ref,
    mix_ref,
    turn_ref,
    sum_ref,
    edge_ref,
):
    modes = table_ref.shape[0] // 4
    forward_tab = table_ref[: 2 * modes, :]
    back = table_ref[2 * modes :, :]
    inverse_tab = back.astype(F32).T.astype(BF)
    near = grad_ref.shape[0]
    cells = near - 2
    bins, chans = grad_ref.shape[1:]
    rows = spec_ref.shape[1]
    band = 32
    core = core_ref[0]
    sum_ref[...] = jnp.zeros_like(sum_ref)
    for edge, column in enumerate((0, near + 3)):
        cot = jnp.sum(wide_ref[column, 0:16, :].astype(F32), 0, keepdims=True)
        edge_ref[edge] = jnp.broadcast_to(cot, (chans, bins)).T
    spec_ref[:, near:, :] = jnp.zeros((2 * modes, rows - near, chans), F32)
    for cell in range(near):
        spec_ref[:, cell, :] = jnp.dot(
            forward_tab, wide_ref[cell + 2], preferred_element_type=F32
        )

    def mix_one(mode, carry):
        lhs = jnp.concatenate([spec_ref[mode], spec_ref[modes + mode]], 0).astype(BF)
        by_real, by_imag = [
            jnp.dot(
                lhs,
                pick_weight(core, got_ref, other_ref, mode, side),
                preferred_element_type=F32,
            )
            for side in range(2)
        ]
        mix_ref[:, mode, :] = by_real[:rows] - by_imag[rows:]
        mix_ref[:, modes + mode, :] = by_imag[:rows] + by_real[rows:]
        return carry

    lax.fori_loop(0, modes, mix_one, 0, unroll=4)

    def one_cell(cell, own, scale_ref, place):
        spectral = jnp.dot(inverse_tab, mix_ref[cell].astype(BF), preferred_element_type=F32)
        pieces = []
        for start in range(0, bins, band):
            span = slice(start, start + band)
            total = spectral[span]
            windows = []
            for row, ref in enumerate((far_ref, wide_ref, close_ref)):
                skip = 1 if row else 0
                for col in range(3):
                    window = ref[cell + col + skip, span, :].astype(F32)
                    windows.append(window)
                    total = total + window * conv_ref[3 * row + col : 3 * row + col + 1, :]
            activ, slope = gelu_pair(total)
            cot = scale_ref[place, span, :]
            grad = (cot * conv_ref[9:10, :] * slope).astype(BF)
            pieces.append(grad)
            if own:
                wide_grad = grad.astype(F32)
                for index_d, window in enumerate(windows + [None]):
                    term = cot * activ if window is None else window * wide_grad
                    sum_ref[index_d] += jnp.sum(term.reshape(band // 8, 8, chans), 0)
        grad = jnp.concatenate(pieces, 0)
        grad_ref[cell] = grad
        return grad

    one_cell(0, False, edge_ref, 0)
    one_cell(near - 1, False, edge_ref, 1)

    def own_cell(cell, carry):
        grad = one_cell(cell + 1, True, cot_ref, cell)
        turn_ref[:, cell, :] = jnp.dot(back, grad, preferred_element_type=F32)
        return carry

    lax.fori_loop(0, cells, own_cell, 0)
    small = [jnp.sum(sum_ref[index_d], 0, keepdims=True) for index_d in range(10)]
    upper, lower = jnp.concatenate(small[:3], 0), jnp.concatenate(small[6:9], 0)
    small = jnp.concatenate(
        [
            jnp.where(core == 0, upper, lower),
            *small[3:6],
            jnp.where(core == 0, lower, upper),
            small[9],
            jnp.zeros((6, chans), F32),
        ],
        0,
    ).astype(BF)

    def pack_one(mode, carry):
        pair = jnp.concatenate([turn_ref[mode], turn_ref[modes + mode]], 0).astype(BF)
        for part in range(2):
            sent_ref[2 * mode + part, 0:16, :] = pair
            sent_ref[2 * mode + part, 16:32, :] = small
        return carry

    lax.fori_loop(0, modes, pack_one, 0, unroll=4)


def last_kernel(
    core_ref,
    got_ref,
    other_ref,
    sent_ref,
    far_ref,
    wide_ref,
    close_ref,
    conv_ref,
    table_ref,
    out_ref,
    stack_ref,
):
    modes = table_ref.shape[0] // 4
    forward_turn = table_ref[: 2 * modes, :].astype(F32).T.astype(BF)
    cells, bins, chans = out_ref.shape
    band = 32
    core = core_ref[0]

    def mix_one(mode, carry):
        lhs = sent_ref[2 * mode, 0:16, :]
        by_real, by_imag = [
            lax.dot_general(
                lhs,
                pick_weight(core, got_ref, other_ref, mode, side),
                (((1,), (1,)), ((), ())),
                preferred_element_type=F32,
            )
            for side in range(2)
        ]
        stack_ref[:, mode, :] = by_real[:cells] + by_imag[cells:]
        stack_ref[:, modes + mode, :] = by_real[cells:] - by_imag[:cells]
        return carry

    lax.fori_loop(0, modes, mix_one, 0, unroll=4)

    def one_cell(cell, carry):
        total = jnp.dot(forward_turn, stack_ref[cell].astype(BF), preferred_element_type=F32)
        for start in range(0, bins, band):
            span = slice(start, start + band)
            part = total[span]
            for row, ref in enumerate((close_ref, wide_ref, far_ref)):
                for col in range(3):
                    window = ref[cell + 2 - col, span, :].astype(F32)
                    part = part + window * conv_ref[3 * row + col : 3 * row + col + 1, :]
            out_ref[cell, span, :] = part
        return carry

    lax.fori_loop(0, cells, one_cell, 0)


def gather_kernel(left_ref, got_ref, out_ref):
    tiles, rows, width = left_ref.shape
    chans = got_ref.shape[2]
    term = lax.dot_general(
        left_ref[...].reshape(tiles * rows, width),
        got_ref[:, :rows, :].reshape(tiles * rows, chans),
        (((0,), (0,)), ((), ())),
        preferred_element_type=F32,
    ).astype(BF)
    total = jnp.sum(got_ref[:, rows:, :].astype(F32), 0)
    pieces = [term]
    for _ in range(3):
        piece = total.astype(BF)
        total = total - piece.astype(F32)
        pieces.append(piece)
    block = jnp.concatenate(pieces, 0)
    for group in range(out_ref.shape[0]):
        out_ref[group] = block


def finish_kernel(last_ref, spectral_ref, conv_ref, proj_ref):
    half, width = spectral_ref.shape
    total = jnp.sum(last_ref[...].astype(F32), 0)
    spectral_ref[:, : width // 2] = total[:half]
    spectral_ref[:, width // 2 :] = total[half : 2 * half]
    rest = total[2 * half :]
    rest = rest[:16] + rest[16:32] + rest[32:]
    conv_ref[...] = rest[:9]
    proj_ref[...] = rest[9:10]


def on_core(kernel, operands, out_shape, scratch=(), scalars=1):
    whole = pl.BlockSpec(memory_space=pltpu.VMEM)
    return pl.pallas_call(
        kernel,
        out_shape=out_shape,
        in_specs=[pl.BlockSpec(memory_space=pltpu.SMEM)] * scalars
        + [whole] * (len(operands) - scalars),
        out_specs=jax.tree.map(lambda _: whole, out_shape),
        scratch_shapes=scratch,
        compiler_params=pltpu.CompilerParams(vmem_limit_bytes=20 * 1024 * 1024),
        cost_estimate=pl.CostEstimate(
            flops=200_000_000, bytes_accessed=12_000_000, transcendentals=400_000
        ),
    )(*operands)


def local(hidden, cotangent, spectral_w, conv_k, proj_w):
    rows_here, cols, bins, chans = hidden.shape
    groups = lax.axis_size("grp")
    tiles = lax.axis_size("tile")
    half = spectral_w.shape[0]
    modes = half * tiles // chans
    parts = chans // half
    cells = rows_here * cols
    core = lax.axis_index("grp") % 2
    which = core.astype(jnp.int32).reshape(1)
    quarter = half // 2
    near = cols + 2
    count = conv_k.shape[0] + 1
    tables = spectral_tables(modes, bins)
    upper, centre, lower = conv_k[:3], conv_k[3:6], conv_k[6:]
    gains = jnp.concatenate(
        [
            jnp.where(core == 0, upper, lower),
            centre,
            jnp.where(core == 0, lower, upper),
            proj_w[None],
            jnp.zeros((6, chans), F32),
        ],
        0,
    )
    own_rows = lax.dynamic_slice_in_dim(spectral_w, core * quarter, quarter, 0)
    own_rows = jnp.concatenate([own_rows[:, :chans], own_rows[:, chans:]], 0)
    sent = (
        to_spec(tables[: 2 * modes], hidden[0])
        .reshape(2, modes, cells, parts, half)
        .transpose(1, 3, 2, 0, 4)
        .reshape(tiles, cells, 2 * half)
    )
    sent = jnp.concatenate([jnp.broadcast_to(own_rows, (tiles,) + own_rows.shape), sent], 1)
    sent, hidden, cotangent = tied(sent, hidden, cotangent)
    got = exchange(sent, "tile")
    head, tail = hidden[0, :2], hidden[0, cols - 2 :]
    tail_cot = edge_pack(split3(cotangent[0, cols - 1]), bins)
    head_cot = edge_pack(split3(cotangent[0, 0]), bins)
    low_t = shifted(jnp.concatenate([tail_cot, tail], 0), "tile", 1)
    high_t = shifted(jnp.concatenate([head, head_cot], 0), "tile", -1)
    far = [across(tail, 1), across(hidden[0], 0), across(head, -1)]
    got, low_t, high_t, far = tied(got, low_t, high_t, far)
    far = jnp.concatenate(far, 0)
    wide = jnp.concatenate([low_t, hidden[0], high_t], 0)
    cot_lanes = jnp.broadcast_to(cotangent[0][:, :, None], (cells, bins, chans))
    other = mate(got)
    close = mate(wide)
    grad_wide, grad_sent = on_core(
        middle_kernel,
        (
            which,
            got,
            other,
            far,
            wide,
            close,
            cot_lanes,
            gains,
            tables,
        ),
        (
            jax.ShapeDtypeStruct((near, bins, chans), BF),
            jax.ShapeDtypeStruct((tiles, 32, chans), BF),
        ),
        [
            pltpu.VMEM((2 * modes, 16, chans), F32),
            pltpu.VMEM((16, 2 * modes, chans), F32),
            pltpu.VMEM((2 * modes, cells, chans), F32),
            pltpu.VMEM((count, 8, chans), F32),
            pltpu.VMEM((2, bins, chans), F32),
        ],
    )
    far_grad = across(grad_wide, 0)
    close_grad = mate(grad_wide)
    got_g = exchange(grad_sent, "tile")
    late, _ = tied(got, grad_sent)
    own_h = late[:, 2 * quarter :]
    got_g, far_grad, close_grad = tied(got_g, far_grad, close_grad)
    lane = lax.broadcasted_iota(jnp.int32, own_h.shape, 2)
    left = jnp.concatenate([jnp.where(lane < half, own_h, -own_h), jnp.roll(own_h, half, 2)], 1)
    last = on_core(
        gather_kernel,
        (left, got_g),
        jax.ShapeDtypeStruct((groups, 2 * half + 48, chans), BF),
        scalars=0,
    )
    grad_hidden = on_core(
        last_kernel,
        (
            which,
            got,
            other,
            grad_sent,
            far_grad,
            grad_wide,
            close_grad,
            gains,
            tables,
        ),
        jax.ShapeDtypeStruct((cells, bins, chans), F32),
        [pltpu.VMEM((cells, 2 * modes, chans), F32)],
    ).reshape(rows_here, cols, bins, chans)
    grad_spectral, grad_conv, grad_proj = on_core(
        finish_kernel,
        (exchange(last, "grp"),),
        (
            jax.ShapeDtypeStruct((half, 2 * chans), F32),
            jax.ShapeDtypeStruct((count - 1, chans), F32),
            jax.ShapeDtypeStruct((1, chans), F32),
        ),
        scalars=0,
    )
    return (grad_hidden, grad_spectral, grad_conv, grad_proj[0])


def solution(mesh):
    in_specs = (P("grp", "tile", None, None), P("grp", "tile", None), P("tile", None), P(), P())
    out_specs = (P("grp", "tile", None, None), P("tile", None), P(), P())
    return jax.shard_map(local, mesh=mesh, in_specs=in_specs, out_specs=out_specs, check_vma=False)
```
